32 devices in a mesh: groups: 2 (over y), chan: 4 (over z), tm: 2 (over x), band: 2 (over core).
Axes of the slice: x: 2, y: 2, z: 4, core: 2. Of those that a mesh axis runs over, the one named last changes fastest.
Arguments:
- recording: float32 [1024, 2048], P(('groups', 'chan'), 'tm'), parts along dimension 0, may hold values from -460 to 460
- tau_index: int32 [1024], P(('groups', 'chan')), parts along dimension 0, may hold values from 0 to 7
- pair_offset: int32 [4, 4], replicated, may hold values from -1 to 3, as said below
Outputs:
- correlations: float32 [8, 4, 3, 128, 128], P(('groups', 'chan'), None, None, ('tm', 'band')), parts along dimension 0
The draws below stay inside these ranges and needn't reach their ends.
There are 2 independent parts, one for each index of `groups`. The reference program is written for one: setup_inputs(seed, part) draws one part's arguments, and reference() takes and returns one part's arrays. A program takes and returns all parts, laid end to end along the dimension named above; an argument that names none is the same for every part. Nothing has to cross between parts.
Inputs may be any that keep to these rules, and one draw needn't show every extreme that they name: pair_offset[i, q] is an offset of 1 to 3 blocks for q below the row's partner count, and -1 from there on; every row has 1 to 4 partners.
All inputs are finite; a program needn't handle non-finite values.
Results may differ from the reference program's by a relative error of at most 0.006.
Values may be sent and summed in bfloat16 or wider, within the bound.
A program may use at most 64 MiB of HBM per device.

```python
import jax
import jax.numpy as jnp
from jax import lax

BLK = 128
HALO_CH = 64
HALO_T = 256
LAGS = 3
QMAX = 4
NTAU = 8
CHANNELS = 512
SAMPLES = 2048
NF = 512
K0 = 128
NB = 4
RB = 1
MAXOFF = 3


def draw_recording(key, part):
    base = jax.random.fold_in(key, 11)
    key_noise, key_chan, key_time = jax.random.split(base, 3)
    chan_scale = 10.0 ** jax.random.uniform(key_chan, (CHANNELS, 1), jnp.float32)
    time_scale = jnp.repeat(10.0 ** jax.random.uniform(key_time, (1, SAMPLES // 32), jnp.float32), 32, axis=1)
    noise = jax.random.truncated_normal(key_noise, -4.0, 4.0, (CHANNELS, SAMPLES), jnp.float32)
    return noise * chan_scale * time_scale


def draw_pair_offset(key, part):
    base = jax.random.fold_in(key, 23)
    key_count, key_row, key_offset, key_far, key_back = jax.random.split(base, 5)
    rows = jnp.arange(NB)
    lottery = jax.random.randint(key_count, (NB,), 0, 4)
    counts = jnp.where(lottery == 0, QMAX, 1)
    busy_row = jax.random.randint(key_row, (), 0, NB)
    far_row = jax.random.randint(key_far, (), 0, NB)
    back_row = jax.random.randint(key_back, (), 0, NB // RB) * RB
    counts = jnp.where((rows == busy_row) | (rows == far_row) | (rows == back_row), QMAX, counts)
    offsets = jax.random.randint(key_offset, (NB, QMAX), 1, MAXOFF + 1)
    slots = jnp.arange(QMAX)[None, :]
    far_slot = (rows[:, None] == far_row) & (slots == 0)
    offsets = jnp.where(far_slot, NB // 2, offsets)
    back_slot = (rows[:, None] == back_row) & (slots == 1)
    offsets = jnp.where(back_slot, MAXOFF, offsets)
    used = slots < counts[:, None]
    return jnp.where(used, offsets, -1).astype(jnp.int32)


def set_ends(values, stream_key, smallest, largest):
    spot = [jax.random.randint(jax.random.fold_in(stream_key, axis), (), 0, length) for axis, length in enumerate(values.shape)]
    widest = values.shape.index(max(values.shape))
    neighbour = spot[:widest] + [(spot[widest] + 1) % values.shape[widest]] + spot[widest + 1:]
    return values.at[tuple(spot)].set(smallest).at[tuple(neighbour)].set(largest)


def setup_inputs(seed: int = 0, part: int = 0) -> dict:
    seeds = jax.random.split(jax.random.key(seed), 4)
    own_keys = jax.random.split(jax.random.fold_in(seeds[3], part), 4)
    recording = draw_recording(jax.random.fold_in(jax.random.fold_in(seeds[3], part), 71), part)
    tau_index = set_ends(jax.random.randint(own_keys[1], (CHANNELS,), 0, NTAU), jax.random.fold_in(own_keys[1], 1), 0, NTAU - 1).astype(jnp.int32)
    pair_offset = draw_pair_offset(jax.random.fold_in(seeds[3], 71), part)
    return dict(recording=recording, tau_index=tau_index, pair_offset=pair_offset)


def window_sum(values, reach, axis):
    widths = [(0, 0), (0, 0)]
    widths[axis] = (reach, reach)
    padded = jnp.pad(values, widths)
    zero_shape = list(padded.shape)
    zero_shape[axis] = 1
    running = jnp.concatenate([jnp.zeros(zero_shape, jnp.float32), jnp.cumsum(padded, axis=axis)], axis=axis)
    size = values.shape[axis]
    upper = lax.slice_in_dim(running, 2 * reach + 1, 2 * reach + 1 + size, axis=axis)
    lower = lax.slice_in_dim(running, 0, size, axis=axis)
    return upper - lower

def reference(recording, tau_index, pair_offset):
    decay = jnp.exp(-1.0 / (2.0 * 2.0 ** (tau_index.astype(jnp.float32) / 2.0)))
    previous = jnp.concatenate([jnp.zeros((CHANNELS, 1), jnp.float32), recording[:, :-1]], axis=1)
    deconv = recording - decay[:, None] * previous
    rows = jnp.arange(CHANNELS)
    counted = (jnp.minimum(rows, HALO_CH) + jnp.minimum(CHANNELS - 1 - rows, HALO_CH) + 1).astype(jnp.float32)
    filtered = deconv - window_sum(deconv, HALO_CH, 0) / counted[:, None]
    amplitude = window_sum(jnp.abs(filtered), HALO_T, 1) / (2.0 * HALO_T + 1.0)
    normed = filtered / (amplitude + 1e-06)
    spectrum = jnp.fft.rfft(normed, axis=1)[:, K0:K0 + NF]
    spec_re = jnp.real(spectrum).astype(jnp.float32)
    spec_im = jnp.imag(spectrum).astype(jnp.float32)
    power = lax.optimization_barrier(jnp.sum(spec_re * spec_re + spec_im * spec_im, axis=1))
    factor = 1.0 / jnp.sqrt(power / NF + 1e-06)
    white = jnp.stack([(spec_re * factor[:, None]).T, (spec_im * factor[:, None]).T], axis=1).astype(jnp.bfloat16)
    bins = K0 + jnp.arange(NF)
    lagged = jnp.arange(LAGS) - LAGS // 2
    phase = 2.0 * jnp.pi / SAMPLES * (bins[:, None] * lagged[None, :] % SAMPLES).astype(jnp.float32)
    cosine = jnp.cos(phase)[:, :, None]
    sine = jnp.sin(phase)[:, :, None]
    white_f = white.astype(jnp.float32)
    real_part = white_f[:, 0, None, :] * cosine - white_f[:, 1, None, :] * sine
    imag_part = white_f[:, 0, None, :] * sine + white_f[:, 1, None, :] * cosine
    shifted = jnp.stack([real_part, imag_part], axis=1).astype(jnp.bfloat16)
    scale = 1.0 / jnp.sqrt(jnp.float32(NF))
    zero_index = jnp.zeros((), jnp.int32)

    def one_block(block):
        block = block.astype(jnp.int32)
        start_col = (block * BLK).astype(jnp.int32)
        left = lax.dynamic_slice(shifted, (zero_index, zero_index, zero_index, start_col), (NF, 2, LAGS, BLK))
        left = left.reshape(2 * NF, LAGS * BLK).astype(jnp.float32)
        results = []
        for slot in range(QMAX):
            offset = pair_offset[block, slot].astype(jnp.int32)
            partner = ((block + jnp.maximum(offset, 0)) % NB).astype(jnp.int32)
            right = lax.dynamic_slice(white, (zero_index, zero_index, (partner * BLK).astype(jnp.int32)), (NF, 2, BLK))
            right = right.reshape(2 * NF, BLK).astype(jnp.float32)
            product = lax.dot_general(left, right, (((0,), (0,)), ((), ())), precision=lax.Precision.HIGHEST, preferred_element_type=jnp.float32)
            results.append(jnp.where(offset >= 0, product * scale, 0.0))
        return jnp.stack(results).reshape(QMAX, LAGS, BLK, BLK)
    return lax.map(one_block, jnp.arange(NB).astype(jnp.int32))
```

```python
import functools
import math

import jax
import jax.numpy as jnp
import ml_dtypes
import numpy as np
from jax import lax
from jax.experimental import pallas as pl
from jax.experimental.pallas import tpu as pltpu
from jax.sharding import PartitionSpec as P

BLK = 128
HALO_CH = 64
HALO_T = 256
LAGS = 3
QMAX = 4
WIN = 2 * HALO_T + 1
OUT_T = 256
BF = jnp.bfloat16
F32 = jnp.float32
NT = (((1,), (1,)), ((), ()))


def tables(samples, all_samples):
    kept = all_samples // 4
    first = kept // 4
    shares = all_samples // samples
    bins = first + np.arange(kept)
    angle = 2.0 * np.pi / all_samples * (np.arange(samples)[:, None] * bins[None, :] % all_samples)
    full = np.concatenate([np.cos(angle), -np.sin(angle)], axis=1).astype(np.float32)
    high = full.astype(ml_dtypes.bfloat16)
    low = (full - high.astype(np.float32)).astype(ml_dtypes.bfloat16)
    turn = 2.0 * np.pi / shares * (np.arange(shares)[:, None] * bins[None, :] % shares)
    share_phase = np.stack([np.cos(turn), np.sin(turn)], axis=1).astype(np.float32)
    lags = np.arange(LAGS) - LAGS // 2
    phase = 2.0 * np.pi / all_samples * (lags[:, None] * bins[None, :] % all_samples)
    lag_phase = np.stack([np.cos(phase), np.sin(phase)], axis=1).astype(np.float32)
    return np.stack([high, low]), share_phase, lag_phase


def split(x):
    high = x.astype(BF)
    return high, (x - high.astype(F32)).astype(BF)


def dot(a, b):
    return jnp.dot(a, b, preferred_element_type=F32)


def kernel(
    C, T, B,
    rec, tau, pair, table_hbm, share_phase, lag_phase, out,
    table, deconv, halo, g_send, g_own, g_halo, wide, filt, spec, parts, white,
    table_sem, send_sem, halo_sem, time_sem, part_sem, z_sem, x_sem, c_sem,
):
    samples = rec.shape[1]
    half = BLK // B
    rows = BLK // (T * B)
    kept = spec.shape[1] // 2
    c = lax.axis_index("chan")
    t = lax.axis_index("tm")
    b = lax.axis_index("band")
    sends = []
    used = [0]

    def remote(src, dst, recv, where, cond=None, at=None):
        if at is None:
            at = used[0]
            used[0] += 1
        copy = pltpu.make_async_remote_copy(
            src_ref=src, dst_ref=dst, send_sem=send_sem.at[at], recv_sem=recv,
            device_id=where, device_id_type=pl.DeviceIdType.MESH,
        )
        return copy, cond

    def start(*args, **kw):
        copy, cond = remote(*args, **kw)
        sends.append((copy, cond))
        if cond is None:
            copy.start()
        else:
            pl.when(cond)(copy.start)

    def arrived(src, dst, recv, cond=None):
        copy, _ = remote(src, dst, recv, {"band": 1 - b}, at=0)
        if cond is None:
            copy.wait_recv()
        else:
            pl.when(cond)(copy.wait_recv)

    fetch = pltpu.make_async_copy(table_hbm, table, table_sem)
    fetch.start()

    barrier = pltpu.get_barrier_semaphore()
    peers = 0
    for dc in range(C):
        for dt in range(T):
            for db in range(B):
                same = dc == 0 and (dt or db)
                line = dc != 0 and dt == 0 and db == 0
                corner = dc in (1, C - 1) and dt in (1, T - 1) and db == 0
                if not (same or line or (corner and dc != 0 and dt != 0)):
                    continue
                peers += 1
                pl.semaphore_signal(
                    barrier, inc=1,
                    device_id={
                        "chan": lax.rem(c + dc, C), "tm": lax.rem(t + dt, T), "band": lax.rem(b + db, B)
                    },
                    device_id_type=pl.DeviceIdType.MESH,
                )

    tau_row = 2.0 * jnp.exp(tau[...].astype(F32) * (0.5 * math.log(2.0)))
    decay = jnp.transpose(jnp.broadcast_to(jnp.exp(-1.0 / tau_row), (BLK, BLK)))
    lane = lax.broadcasted_iota(jnp.int32, (BLK, BLK), 1)
    last = rec[:, samples - BLK :]
    g_send[...] = jnp.transpose(decay * last)[BLK - 8 :, :]
    decay_wide = jnp.concatenate([decay] * (samples // BLK), axis=1)
    x = rec[...]
    before = pltpu.roll(x, 1, 1)
    first_col = lax.broadcasted_iota(jnp.int32, x.shape, 1) == 0
    deconv[...] = x - jnp.where(first_col, 0.0, decay_wide * before)

    pl.semaphore_wait(barrier, peers)

    step = 1 - 2 * b
    to_chan = c + step
    from_chan = c - step
    has_to = (to_chan >= 0) & (to_chan < C)
    has_from = (from_chan >= 0) & (from_chan < C)
    to_safe = jnp.clip(to_chan, 0, C - 1)
    near = pl.ds(pl.multiple_of((1 - b) * half, half), half)
    start(deconv.at[near], halo, halo_sem.at[0], {"chan": to_safe}, has_to)
    t_next = jnp.minimum(t + 1, T - 1)
    t_prev = jnp.maximum(t - 1, 0)
    has_next = t < T - 1
    has_prev = t > 0
    start(g_send, g_own, halo_sem.at[1], {"tm": t_next}, has_next)
    start(g_send, g_halo, halo_sem.at[2], {"tm": t_next, "chan": to_safe}, has_next & has_to)

    i_own = lax.broadcasted_iota(jnp.int32, (half, BLK), 0) + b * half
    j_own = lax.broadcasted_iota(jnp.int32, (half, BLK), 1)
    near_own = (jnp.abs(i_own - j_own) <= HALO_CH).astype(F32).astype(BF)
    i_h = lax.broadcasted_iota(jnp.int32, (half, half), 0)
    j_h = lax.broadcasted_iota(jnp.int32, (half, half), 1)
    near_halo = (((j_h - i_h) * step) >= 0).astype(F32).astype(BF)
    m = lax.broadcasted_iota(jnp.int32, (OUT_T + 2 * HALO_T, OUT_T), 0)
    o = lax.broadcasted_iota(jnp.int32, (OUT_T + 2 * HALO_T, OUT_T), 1)
    window = ((m >= o) & (m <= o + 2 * HALO_T)).astype(F32).astype(BF)
    all_channels = BLK * C
    r_global = lax.broadcasted_iota(jnp.int32, (half, samples), 0) + c * BLK + b * half
    counted = jnp.minimum(r_global, HALO_CH) + jnp.minimum(all_channels - 1 - r_global, HALO_CH) + 1
    per_count = 1.0 / counted.astype(F32)

    @pl.when(jnp.logical_not(has_from))
    def _():
        halo[...] = jnp.zeros_like(halo)

    @pl.when(jnp.logical_not(has_prev))
    def _():
        g_own[...] = jnp.zeros_like(g_own)
        wide[:, :HALO_T] = jnp.zeros((half, HALO_T), BF)

    @pl.when(jnp.logical_not(has_prev & has_from))
    def _():
        g_halo[...] = jnp.zeros_like(g_halo)

    @pl.when(jnp.logical_not(has_next))
    def _():
        wide[:, HALO_T + samples :] = jnp.zeros((half, HALO_T), BF)

    arrived(g_send, g_own, halo_sem.at[1], has_prev)
    arrived(g_send, g_halo, halo_sem.at[2], has_prev & has_from)
    lane0 = lane == 0

    def column(g):
        return jnp.where(lane0, jnp.transpose(jnp.broadcast_to(g[7:8, :], (BLK, BLK))), 0.0)

    fix_own = column(g_own[...])
    fix_halo_all = column(g_halo[...])
    fix_halo = jnp.where(b == 0, fix_halo_all[half:, :], fix_halo_all[:half, :])
    d = deconv[...]
    d = jnp.concatenate([d[:, :BLK] - fix_own, d[:, BLK:]], axis=1)
    d_high, d_low = split(d)
    total = dot(near_own, d_high) + dot(near_own, d_low)
    mine = jnp.where(b == 0, d[:half], d[half:])

    arrived(deconv.at[near], halo, halo_sem.at[0], has_from)
    h = halo[...]
    h = jnp.concatenate([h[:, :BLK] - fix_halo, h[:, BLK:]], axis=1)
    h_high, h_low = split(h)
    total = total + dot(near_halo, h_high) + dot(near_halo, h_low)
    filtered = mine - total * per_count
    filt[...] = filtered
    wide[:, HALO_T : HALO_T + samples] = jnp.abs(filtered).astype(BF)

    start(
        wide.at[:, pl.ds(samples, HALO_T)], wide.at[:, pl.ds(0, HALO_T)],
        time_sem.at[0], {"tm": t_next}, has_next,
    )
    start(
        wide.at[:, pl.ds(HALO_T, HALO_T)], wide.at[:, pl.ds(HALO_T + samples, HALO_T)],
        time_sem.at[1], {"tm": t_prev}, has_prev,
    )

    def normed_block(n):
        at = n * OUT_T
        amp = dot(wide[:, at : at + OUT_T + 2 * HALO_T], window)
        return filt[:, at : at + OUT_T] / (amp * (1.0 / WIN) + 1e-06)

    blocks = samples // OUT_T
    inner = [normed_block(n) for n in range(1, blocks - 1)]
    fetch.wait()
    arrived(
        wide.at[:, pl.ds(samples, HALO_T)], wide.at[:, pl.ds(0, HALO_T)], time_sem.at[0], has_prev
    )
    arrived(
        wide.at[:, pl.ds(HALO_T, HALO_T)], wide.at[:, pl.ds(HALO_T + samples, HALO_T)],
        time_sem.at[1], has_next,
    )
    normed = jnp.concatenate([normed_block(0)] + inner + [normed_block(blocks - 1)], axis=1)
    n_high, n_low = split(normed)
    both = dot(jnp.concatenate([n_high, n_low], axis=0), table[0])
    spectrum = both[:half] + both[half:] + dot(n_high, table[1])
    cos_t = share_phase[t, 0:1, :]
    sin_t = share_phase[t, 1:2, :]
    re, im = spectrum[:, :kept], spectrum[:, kept:]
    spec[:, :kept] = (re * cos_t + im * sin_t).astype(BF)
    spec[:, kept:] = (im * cos_t - re * sin_t).astype(BF)

    for n in range(T):
        piece = b * T + n
        t_own, b_own = lax.div(piece, B), lax.rem(piece, B)
        me = (t_own == t) & (b_own == b)

        @pl.when(me)
        def _():
            parts[t] = spec[n * rows : (n + 1) * rows, :]

        start(
            spec.at[pl.ds(n * rows, rows)], parts.at[t], part_sem.at[t],
            {"tm": t_own, "band": b_own}, jnp.logical_not(me),
        )
    own = t * B + b
    b_from = lax.div(own, T)
    for n in range(T):
        arrived(
            spec.at[pl.ds(0, rows)], parts.at[n], part_sem.at[n],
            jnp.logical_not((t == n) & (b_from == b)),
        )
    spectra = parts[0].astype(F32)
    for n in range(1, T):
        spectra = spectra + parts[n].astype(F32)
    power = jnp.sum(spectra * spectra, axis=1, keepdims=True)
    mine_white = (spectra * lax.rsqrt(power * (1.0 / kept) + 1e-06)).astype(BF)
    white[c, own] = mine_white

    order = [d for pair_d in zip(range(1, C), range(C - 1, 0, -1)) for d in pair_d]
    order = list(dict.fromkeys(order))
    for dc in order:
        start(white.at[c, own], white.at[c, own], z_sem.at[c], {"chan": lax.rem(c + dc, C)})
    w = mine_white.astype(F32)
    wr, wi = w[:, :kept], w[:, kept:]
    left = []
    for lag in range(LAGS):
        cos_l = lag_phase[lag, 0:1, :]
        sin_l = lag_phase[lag, 1:2, :]
        left.append(jnp.concatenate([wr * cos_l - wi * sin_l, wr * sin_l + wi * cos_l], axis=1))
    left = jnp.concatenate(left, axis=0).astype(BF)
    for dc in order:
        p = lax.rem(c + dc, C)
        arrived(white.at[p, own], white.at[p, own], z_sem.at[p])
        for dt in range(1, T):
            start(
                white.at[p, own], white.at[p, own], x_sem.at[p, t], {"tm": lax.rem(t + dt, T)}
            )
        start(white.at[p, own], white.at[p, own], c_sem.at[p, t], {"band": 1 - b})
    for dc in order:
        p = lax.rem(c + dc, C)
        for dt in range(1, T):
            tt = lax.rem(t + dt, T)
            at = tt * B + b
            arrived(white.at[p, at], white.at[p, at], x_sem.at[p, tt])
            start(white.at[p, at], white.at[p, at], c_sem.at[p, tt], {"band": 1 - b})
    for dc in order:
        p = lax.rem(c + dc, C)
        for tt in range(T):
            at = tt * B + (1 - b)
            arrived(white.at[p, at], white.at[p, at], c_sem.at[p, tt])

    scale = 1.0 / math.sqrt(kept)
    for q in range(QMAX):
        offset = pair[c, q]
        present = offset >= 0
        p = lax.rem(c + jnp.where(present, offset, 1), C)
        right = white[p].reshape(BLK, 2 * kept)
        product = lax.dot_general(left, right, NT, preferred_element_type=F32)
        product = jnp.where(present, product * scale, 0.0)
        for lag in range(LAGS):
            out[0, q, lag] = product[lag * rows : (lag + 1) * rows]

    for copy, cond in sends:
        if cond is None:
            copy.wait_send()
        else:
            pl.when(cond)(copy.wait_send)


def shards(recording, tau_index, pair_offset):
    channels, samples = recording.shape
    C = lax.axis_size("chan")
    T = lax.axis_size("tm")
    B = lax.axis_size("band")
    all_samples = samples * T
    kept = all_samples // 4
    half = BLK // B
    rows = BLK // (T * B)
    table, share_phase, lag_phase = tables(samples, all_samples)
    vmem = pl.BlockSpec(memory_space=pltpu.VMEM)
    n_send = 3 + 2 + T + (C - 1) * (1 + T + T) + 4
    need = table.nbytes + C * BLK * 2 * kept * 2
    return pl.pallas_call(
        functools.partial(kernel, C, T, B),
        out_shape=jax.ShapeDtypeStruct((1, QMAX, LAGS, rows, BLK), F32),
        in_specs=[
            vmem, vmem, pl.BlockSpec(memory_space=pltpu.SMEM),
            pl.BlockSpec(memory_space=pl.ANY), vmem, vmem,
        ],
        out_specs=vmem,
        scratch_shapes=[
            pltpu.VMEM(table.shape, BF),
            pltpu.VMEM((BLK, samples), F32),
            pltpu.VMEM((half, samples), F32),
            pltpu.VMEM((8, BLK), F32),
            pltpu.VMEM((8, BLK), F32),
            pltpu.VMEM((8, BLK), F32),
            pltpu.VMEM((half, samples + 2 * HALO_T), BF),
            pltpu.VMEM((half, samples), F32),
            pltpu.VMEM((half, 2 * kept), BF),
            pltpu.VMEM((T, rows, 2 * kept), BF),
            pltpu.VMEM((C, T * B, rows, 2 * kept), BF),
            pltpu.SemaphoreType.DMA,
            pltpu.SemaphoreType.DMA((n_send,)),
            pltpu.SemaphoreType.DMA((3,)),
            pltpu.SemaphoreType.DMA((2,)),
            pltpu.SemaphoreType.DMA((T,)),
            pltpu.SemaphoreType.DMA((C,)),
            pltpu.SemaphoreType.DMA((C, T)),
            pltpu.SemaphoreType.DMA((C, T)),
        ],
        compiler_params=pltpu.CompilerParams(
            collective_id=0, has_side_effects=True, vmem_limit_bytes=need + (20 << 20)
        ),
    )(
        recording, tau_index.reshape(1, channels), pair_offset,
        jnp.asarray(table), jnp.asarray(share_phase), jnp.asarray(lag_phase),
    )


def solution(mesh):
    return jax.shard_map(
        shards,
        mesh=mesh,
        in_specs=(P(("groups", "chan"), "tm"), P(("groups", "chan")), P()),
        out_specs=P(("groups", "chan"), None, None, ("tm", "band"), None),
        check_vma=False,
    )
```

```python
import functools
import math

import jax
import jax.numpy as jnp
import ml_dtypes
import numpy as np
from jax import lax
from jax.experimental import pallas as pl
from jax.experimental.pallas import tpu as pltpu
from jax.sharding import PartitionSpec as P

BLK = 128
HALO_CH = 64
HALO_T = 256
LAGS = 3
QMAX = 4
WIN = 2 * HALO_T + 1
OUT_T = 256
BF = jnp.bfloat16
F32 = jnp.float32
NT = (((1,), (1,)), ((), ()))


def tables(samples, all_samples):
    kept = all_samples // 4
    first = kept // 4
    shares = all_samples // samples
    bins = first + np.arange(kept)
    angle = 2.0 * np.pi / all_samples * (np.arange(samples)[:, None] * bins[None, :] % all_samples)
    full = np.concatenate([np.cos(angle), -np.sin(angle)], axis=1).astype(np.float32)
    high = full.astype(ml_dtypes.bfloat16)
    low = (full - high.astype(np.float32)).astype(ml_dtypes.bfloat16)
    turn = 2.0 * np.pi / shares * (np.arange(shares)[:, None] * bins[None, :] % shares)
    share_phase = np.stack([np.cos(turn), np.sin(turn)], axis=1).astype(np.float32)
    lags = np.arange(LAGS) - LAGS // 2
    phase = 2.0 * np.pi / all_samples * (lags[:, None] * bins[None, :] % all_samples)
    lag_phase = np.stack([np.cos(phase), np.sin(phase)], axis=1).astype(np.float32)
    return np.stack([high, low]), share_phase, lag_phase


def split(x):
    high = x.astype(BF)
    return high, (x - high.astype(F32)).astype(BF)


def dot(a, b):
    return jnp.dot(a, b, preferred_element_type=F32)


def kernel(
    C, T, B,
    rec, tau, pair, table_hbm, share_phase, lag_phase, out,
    table, deconv, halo, g_send, g_own, g_halo, wide, filt, spec, parts, white,
    table_sem, send_sem, halo_sem, time_sem, part_sem, z_sem, x_sem, c_sem,
):
    samples = rec.shape[1]
    half = BLK // B
    rows = BLK // (T * B)
    kept = spec.shape[1] // 2
    c = lax.axis_index("chan")
    t = lax.axis_index("tm")
    b = lax.axis_index("band")
    sends = []
    used = [0]

    def remote(src, dst, recv, where, cond=None, at=None):
        if at is None:
            at = used[0]
            used[0] += 1
        copy = pltpu.make_async_remote_copy(
            src_ref=src, dst_ref=dst, send_sem=send_sem.at[at], recv_sem=recv,
            device_id=where, device_id_type=pl.DeviceIdType.MESH,
        )
        return copy, cond

    def start(*args, **kw):
        copy, cond = remote(*args, **kw)
        sends.append((copy, cond))
        if cond is None:
            copy.start()
        else:
            pl.when(cond)(copy.start)

    def arrived(src, dst, recv, cond=None):
        copy, _ = remote(src, dst, recv, {"band": 1 - b}, at=0)
        if cond is None:
            copy.wait_recv()
        else:
            pl.when(cond)(copy.wait_recv)

    fetch = pltpu.make_async_copy(table_hbm, table, table_sem)
    fetch.start()

    barrier = pltpu.get_barrier_semaphore()
    peers = T * B - 1
    for other in range(1, T * B):
        dt, db = divmod(other, B)
        pl.semaphore_signal(
            barrier, inc=1, device_id={"tm": lax.rem(t + dt, T), "band": lax.rem(b + db, B)},
            device_id_type=pl.DeviceIdType.MESH,
        )
    for dc in [x for x in range(1 - C, C) if x]:
        for dt in (-1, 0, 1) if abs(dc) == 1 else (0,):
            there = (c + dc >= 0) & (c + dc < C) & (t + dt >= 0) & (t + dt < T)
            peers = peers + there.astype(jnp.int32)

            @pl.when(there)
            def _():
                pl.semaphore_signal(
                    barrier, inc=1,
                    device_id={
                        "chan": jnp.clip(c + dc, 0, C - 1), "tm": jnp.clip(t + dt, 0, T - 1)
                    },
                    device_id_type=pl.DeviceIdType.MESH,
                )

    tau_row = 2.0 * jnp.exp(tau[...].astype(F32) * (0.5 * math.log(2.0)))
    decay = jnp.transpose(jnp.broadcast_to(jnp.exp(-1.0 / tau_row), (BLK, BLK)))
    lane = lax.broadcasted_iota(jnp.int32, (BLK, BLK), 1)
    last = rec[:, samples - BLK :]
    g_send[...] = jnp.transpose(decay * last)[BLK - 8 :, :]
    decay_wide = jnp.concatenate([decay] * (samples // BLK), axis=1)
    x = rec[...]
    before = pltpu.roll(x, 1, 1)
    first_col = lax.broadcasted_iota(jnp.int32, x.shape, 1) == 0
    deconv[...] = x - jnp.where(first_col, 0.0, decay_wide * before)

    pl.semaphore_wait(barrier, peers)

    step = 1 - 2 * b
    to_chan = c + step
    from_chan = c - step
    has_to = (to_chan >= 0) & (to_chan < C)
    has_from = (from_chan >= 0) & (from_chan < C)
    to_safe = jnp.clip(to_chan, 0, C - 1)
    near = pl.ds(pl.multiple_of((1 - b) * half, half), half)
    start(deconv.at[near], halo, halo_sem.at[0], {"chan": to_safe}, has_to)
    t_next = jnp.minimum(t + 1, T - 1)
    t_prev = jnp.maximum(t - 1, 0)
    has_next = t < T - 1
    has_prev = t > 0
    start(g_send, g_own, halo_sem.at[1], {"tm": t_next}, has_next)
    start(g_send, g_halo, halo_sem.at[2], {"tm": t_next, "chan": to_safe}, has_next & has_to)

    i_own = lax.broadcasted_iota(jnp.int32, (half, BLK), 0) + b * half
    j_own = lax.broadcasted_iota(jnp.int32, (half, BLK), 1)
    near_own = (jnp.abs(i_own - j_own) <= HALO_CH).astype(F32).astype(BF)
    i_h = lax.broadcasted_iota(jnp.int32, (half, half), 0)
    j_h = lax.broadcasted_iota(jnp.int32, (half, half), 1)
    near_halo = (((j_h - i_h) * step) >= 0).astype(F32).astype(BF)
    m = lax.broadcasted_iota(jnp.int32, (OUT_T + 2 * HALO_T, OUT_T), 0)
    o = lax.broadcasted_iota(jnp.int32, (OUT_T + 2 * HALO_T, OUT_T), 1)
    window = ((m >= o) & (m <= o + 2 * HALO_T)).astype(F32).astype(BF)
    all_channels = BLK * C
    r_global = lax.broadcasted_iota(jnp.int32, (half, samples), 0) + c * BLK + b * half
    counted = jnp.minimum(r_global, HALO_CH) + jnp.minimum(all_channels - 1 - r_global, HALO_CH) + 1
    per_count = 1.0 / counted.astype(F32)

    @pl.when(jnp.logical_not(has_from))
    def _():
        halo[...] = jnp.zeros_like(halo)

    @pl.when(jnp.logical_not(has_prev))
    def _():
        g_own[...] = jnp.zeros_like(g_own)
        wide[:, :HALO_T] = jnp.zeros((half, HALO_T), BF)

    @pl.when(jnp.logical_not(has_prev & has_from))
    def _():
        g_halo[...] = jnp.zeros_like(g_halo)

    @pl.when(jnp.logical_not(has_next))
    def _():
        wide[:, HALO_T + samples :] = jnp.zeros((half, HALO_T), BF)

    arrived(g_send, g_own, halo_sem.at[1], has_prev)
    arrived(g_send, g_halo, halo_sem.at[2], has_prev & has_from)
    lane0 = lane == 0

    def column(g):
        return jnp.where(lane0, jnp.transpose(jnp.broadcast_to(g[7:8, :], (BLK, BLK))), 0.0)

    fix_own = column(g_own[...])
    fix_halo_all = column(g_halo[...])
    fix_halo = jnp.where(b == 0, fix_halo_all[half:, :], fix_halo_all[:half, :])
    d = deconv[...]
    d = jnp.concatenate([d[:, :BLK] - fix_own, d[:, BLK:]], axis=1)
    d_high, d_low = split(d)
    total = dot(near_own, d_high) + dot(near_own, d_low)
    mine = jnp.where(b == 0, d[:half], d[half:])

    arrived(deconv.at[near], halo, halo_sem.at[0], has_from)
    h = halo[...]
    h = jnp.concatenate([h[:, :BLK] - fix_halo, h[:, BLK:]], axis=1)
    h_high, h_low = split(h)
    total = total + dot(near_halo, h_high) + dot(near_halo, h_low)
    filtered = mine - total * per_count
    filt[...] = filtered
    wide[:, HALO_T : HALO_T + samples] = jnp.abs(filtered).astype(BF)

    start(
        wide.at[:, pl.ds(samples, HALO_T)], wide.at[:, pl.ds(0, HALO_T)],
        time_sem.at[0], {"tm": t_next}, has_next,
    )
    start(
        wide.at[:, pl.ds(HALO_T, HALO_T)], wide.at[:, pl.ds(HALO_T + samples, HALO_T)],
        time_sem.at[1], {"tm": t_prev}, has_prev,
    )

    def normed_block(n):
        at = n * OUT_T
        amp = dot(wide[:, at : at + OUT_T + 2 * HALO_T], window)
        return filt[:, at : at + OUT_T] / (amp * (1.0 / WIN) + 1e-06)

    blocks = samples // OUT_T
    inner = [normed_block(n) for n in range(1, blocks - 1)]
    fetch.wait()
    arrived(
        wide.at[:, pl.ds(samples, HALO_T)], wide.at[:, pl.ds(0, HALO_T)], time_sem.at[0], has_prev
    )
    arrived(
        wide.at[:, pl.ds(HALO_T, HALO_T)], wide.at[:, pl.ds(HALO_T + samples, HALO_T)],
        time_sem.at[1], has_next,
    )
    normed = jnp.concatenate([normed_block(0)] + inner + [normed_block(blocks - 1)], axis=1)
    n_high, n_low = split(normed)
    both = dot(jnp.concatenate([n_high, n_low], axis=0), table[0])
    spectrum = both[:half] + both[half:] + dot(n_high, table[1])
    cos_t = share_phase[t, 0:1, :]
    sin_t = share_phase[t, 1:2, :]
    re, im = spectrum[:, :kept], spectrum[:, kept:]
    spec[:, :kept] = (re * cos_t + im * sin_t).astype(BF)
    spec[:, kept:] = (im * cos_t - re * sin_t).astype(BF)

    for n in range(T):
        piece = b * T + n
        t_own, b_own = lax.div(piece, B), lax.rem(piece, B)
        me = (t_own == t) & (b_own == b)

        @pl.when(me)
        def _():
            parts[t] = spec[n * rows : (n + 1) * rows, :]

        start(
            spec.at[pl.ds(n * rows, rows)], parts.at[t], part_sem.at[t],
            {"tm": t_own, "band": b_own}, jnp.logical_not(me),
        )
    own = t * B + b
    b_from = lax.div(own, T)
    for n in range(T):
        arrived(
            spec.at[pl.ds(0, rows)], parts.at[n], part_sem.at[n],
            jnp.logical_not((t == n) & (b_from == b)),
        )
    spectra = parts[0].astype(F32)
    for n in range(1, T):
        spectra = spectra + parts[n].astype(F32)
    power = jnp.sum(spectra * spectra, axis=1, keepdims=True)
    mine_white = (spectra * lax.rsqrt(power * (1.0 / kept) + 1e-06)).astype(BF)
    white[c, own] = mine_white

    up, down = jnp.minimum(c + 1, C - 1), jnp.maximum(c - 1, 0)
    for n in range(1, C):
        for sign in (-1, 1):
            to = c + sign * n
            start(
                white.at[c, own], white.at[c, own], z_sem.at[c],
                {"chan": jnp.clip(to, 0, C - 1)}, (to >= 0) & (to < C),
            )

    def block_at(n, sign):
        block = c + sign * n
        return (block >= 0) & (block < C), jnp.clip(block, 0, C - 1)

    def across(n, sign):
        there, p = block_at(n, sign)
        for dt in range(1, T):
            tt = lax.rem(t + dt, T)
            piece = white.at[p, tt * B + b]
            arrived(piece, piece, x_sem.at[p, tt], there)
            start(piece, piece, c_sem.at[p, tt], {"band": 1 - b}, there)

    w = mine_white.astype(F32)
    wr, wi = w[:, :kept], w[:, kept:]
    left = []
    for lag in range(LAGS):
        cos_l = lag_phase[lag, 0:1, :]
        sin_l = lag_phase[lag, 1:2, :]
        left.append(jnp.concatenate([wr * cos_l - wi * sin_l, wr * sin_l + wi * cos_l], axis=1))
    left = jnp.concatenate(left, axis=0).astype(BF)
    steps = [(n, sign) for n in range(1, C) for sign in (-1, 1)]
    for n in range(1, C):
        for sign in (-1, 1):
            there, p = block_at(n, sign)
            piece = white.at[p, own]
            arrived(piece, piece, z_sem.at[p], there)
            for dt in range(1, T):
                start(piece, piece, x_sem.at[p, t], {"tm": lax.rem(t + dt, T)}, there)
            start(piece, piece, c_sem.at[p, t], {"band": 1 - b}, there)
        if n > 2:
            for sign in (-1, 1):
                across(n - 2, sign)
    for sign in (-1, 1):
        if C > 2:
            across(C - 2, sign)
    for sign in (-1, 1):
        across(C - 1, sign)
    for n, sign in steps:
        there, p = block_at(n, sign)
        for tt in range(T):
            piece = white.at[p, tt * B + (1 - b)]
            arrived(piece, piece, c_sem.at[p, tt], there)

    scale = 1.0 / math.sqrt(kept)
    for q in range(QMAX):
        offset = pair[c, q]
        present = offset >= 0
        p = lax.rem(c + jnp.where(present, offset, 1), C)
        right = white[p].reshape(BLK, 2 * kept)
        product = lax.dot_general(left, right, NT, preferred_element_type=F32)
        product = jnp.where(present, product * scale, 0.0)
        for lag in range(LAGS):
            out[0, q, lag] = product[lag * rows : (lag + 1) * rows]

    for copy, cond in sends:
        if cond is None:
            copy.wait_send()
        else:
            pl.when(cond)(copy.wait_send)


def shards(recording, tau_index, pair_offset):
    channels, samples = recording.shape
    C = lax.axis_size("chan")
    T = lax.axis_size("tm")
    B = lax.axis_size("band")
    all_samples = samples * T
    kept = all_samples // 4
    half = BLK // B
    rows = BLK // (T * B)
    table, share_phase, lag_phase = tables(samples, all_samples)
    vmem = pl.BlockSpec(memory_space=pltpu.VMEM)
    n_send = 5 + T + 2 + 2 * (C - 1) * 2 * T
    return pl.pallas_call(
        functools.partial(kernel, C, T, B),
        out_shape=jax.ShapeDtypeStruct((1, QMAX, LAGS, rows, BLK), F32),
        in_specs=[
            vmem, vmem, pl.BlockSpec(memory_space=pltpu.SMEM),
            pl.BlockSpec(memory_space=pl.ANY), vmem, vmem,
        ],
        out_specs=vmem,
        scratch_shapes=[
            pltpu.VMEM(table.shape, BF),
            pltpu.VMEM((BLK, samples), F32),
            pltpu.VMEM((half, samples), F32),
            pltpu.VMEM((8, BLK), F32),
            pltpu.VMEM((8, BLK), F32),
            pltpu.VMEM((8, BLK), F32),
            pltpu.VMEM((half, samples + 2 * HALO_T), BF),
            pltpu.VMEM((half, samples), F32),
            pltpu.VMEM((half, 2 * kept), BF),
            pltpu.VMEM((T, rows, 2 * kept), BF),
            pltpu.VMEM((C, T * B, rows, 2 * kept), BF),
            pltpu.SemaphoreType.DMA,
            pltpu.SemaphoreType.DMA((n_send,)),
            pltpu.SemaphoreType.DMA((3,)),
            pltpu.SemaphoreType.DMA((2,)),
            pltpu.SemaphoreType.DMA((T,)),
            pltpu.SemaphoreType.DMA((C,)),
            pltpu.SemaphoreType.DMA((C, T)),
            pltpu.SemaphoreType.DMA((C, T)),
        ],
        compiler_params=pltpu.CompilerParams(
            collective_id=0, has_side_effects=True, vmem_limit_bytes=61 << 20
        ),
    )(
        recording, tau_index.reshape(1, channels), pair_offset,
        jnp.asarray(table), jnp.asarray(share_phase), jnp.asarray(lag_phase),
    )


def solution(mesh):
    return jax.shard_map(
        shards,
        mesh=mesh,
        in_specs=(P(("groups", "chan"), "tm"), P(("groups", "chan")), P()),
        out_specs=P(("groups", "chan"), None, None, ("tm", "band"), None),
        check_vma=False,
    )
```

```python
import functools
import math

import jax
import jax.numpy as jnp
import ml_dtypes
import numpy as np
from jax import lax
from jax.experimental import pallas as pl
from jax.experimental.pallas import tpu as pltpu
from jax.sharding import PartitionSpec as P

BLK = 128
HALO_CH = 64
HALO_T = 256
LAGS = 3
QMAX = 4
WIN = 2 * HALO_T + 1
OUT_T = 256
BF = jnp.bfloat16
F32 = jnp.float32
NT = (((1,), (1,)), ((), ()))


def tables(samples, all_samples):
    kept = all_samples // 4
    first = kept // 4
    shares = all_samples // samples
    bins = first + np.arange(kept)
    angle = 2.0 * np.pi / all_samples * (np.arange(samples)[:, None] * bins[None, :] % all_samples)
    full = np.concatenate([np.cos(angle), -np.sin(angle)], axis=1).astype(np.float32)
    high = full.astype(ml_dtypes.bfloat16)
    low = (full - high.astype(np.float32)).astype(ml_dtypes.bfloat16)
    turn = 2.0 * np.pi / shares * (np.arange(shares)[:, None] * bins[None, :] % shares)
    share_phase = np.stack([np.cos(turn), np.sin(turn)], axis=1).astype(np.float32)
    lags = np.arange(LAGS) - LAGS // 2
    phase = 2.0 * np.pi / all_samples * (lags[:, None] * bins[None, :] % all_samples)
    lag_phase = np.stack([np.cos(phase), np.sin(phase)], axis=1).astype(np.float32)
    return np.stack([high, low]), share_phase, lag_phase


def split(x):
    high = x.astype(BF)
    return high, (x - high.astype(F32)).astype(BF)


def dot(a, b):
    return jnp.dot(a, b, preferred_element_type=F32)


def kernel(
    C, T, B,
    rec, tau, pair, table_hbm, share_phase, lag_phase, out,
    table, deconv, halo, g_send, g_own, g_halo, wide, filt, spec, parts, white,
    table_sem, send_sem, halo_sem, time_sem, part_sem, z_sem, x_sem, c_sem,
):
    samples = rec.shape[1]
    half = BLK // B
    rows = BLK // (T * B)
    kept = spec.shape[1] // 2
    c = lax.axis_index("chan")
    t = lax.axis_index("tm")
    b = lax.axis_index("band")
    sends = []
    used = [0]

    def remote(src, dst, recv, where, cond=None, at=None):
        if at is None:
            at = used[0]
            used[0] += 1
        copy = pltpu.make_async_remote_copy(
            src_ref=src, dst_ref=dst, send_sem=send_sem.at[at], recv_sem=recv,
            device_id=where, device_id_type=pl.DeviceIdType.MESH,
        )
        return copy, cond

    def start(*args, **kw):
        copy, cond = remote(*args, **kw)
        sends.append((copy, cond))
        if cond is None:
            copy.start()
        else:
            pl.when(cond)(copy.start)

    def arrived(src, dst, recv, cond=None):
        copy, _ = remote(src, dst, recv, {"band": 1 - b}, at=0)
        if cond is None:
            copy.wait_recv()
        else:
            pl.when(cond)(copy.wait_recv)

    fetch = pltpu.make_async_copy(table_hbm, table, table_sem)
    fetch.start()

    barrier = pltpu.get_barrier_semaphore()
    peers = T * B - 1
    for other in range(1, T * B):
        dt, db = divmod(other, B)
        pl.semaphore_signal(
            barrier, inc=1, device_id={"tm": lax.rem(t + dt, T), "band": lax.rem(b + db, B)},
            device_id_type=pl.DeviceIdType.MESH,
        )
    for dc in (-2, -1, 1, 2):
        for dt in (-1, 0, 1) if abs(dc) == 1 else (0,):
            there = (c + dc >= 0) & (c + dc < C) & (t + dt >= 0) & (t + dt < T)
            peers = peers + there.astype(jnp.int32)

            @pl.when(there)
            def _():
                pl.semaphore_signal(
                    barrier, inc=1,
                    device_id={
                        "chan": jnp.clip(c + dc, 0, C - 1), "tm": jnp.clip(t + dt, 0, T - 1)
                    },
                    device_id_type=pl.DeviceIdType.MESH,
                )

    tau_row = 2.0 * jnp.exp(tau[...].astype(F32) * (0.5 * math.log(2.0)))
    decay = jnp.transpose(jnp.broadcast_to(jnp.exp(-1.0 / tau_row), (BLK, BLK)))
    lane = lax.broadcasted_iota(jnp.int32, (BLK, BLK), 1)
    last = rec[:, samples - BLK :]
    g_send[...] = jnp.transpose(decay * last)[BLK - 8 :, :]
    decay_wide = jnp.concatenate([decay] * (samples // BLK), axis=1)
    x = rec[...]
    before = pltpu.roll(x, 1, 1)
    first_col = lax.broadcasted_iota(jnp.int32, x.shape, 1) == 0
    deconv[...] = x - jnp.where(first_col, 0.0, decay_wide * before)

    pl.semaphore_wait(barrier, peers)

    step = 1 - 2 * b
    to_chan = c + step
    from_chan = c - step
    has_to = (to_chan >= 0) & (to_chan < C)
    has_from = (from_chan >= 0) & (from_chan < C)
    to_safe = jnp.clip(to_chan, 0, C - 1)
    near = pl.ds(pl.multiple_of((1 - b) * half, half), half)
    start(deconv.at[near], halo, halo_sem.at[0], {"chan": to_safe}, has_to)
    t_next = jnp.minimum(t + 1, T - 1)
    t_prev = jnp.maximum(t - 1, 0)
    has_next = t < T - 1
    has_prev = t > 0
    start(g_send, g_own, halo_sem.at[1], {"tm": t_next}, has_next)
    start(g_send, g_halo, halo_sem.at[2], {"tm": t_next, "chan": to_safe}, has_next & has_to)

    i_own = lax.broadcasted_iota(jnp.int32, (half, BLK), 0) + b * half
    j_own = lax.broadcasted_iota(jnp.int32, (half, BLK), 1)
    near_own = (jnp.abs(i_own - j_own) <= HALO_CH).astype(F32).astype(BF)
    i_h = lax.broadcasted_iota(jnp.int32, (half, half), 0)
    j_h = lax.broadcasted_iota(jnp.int32, (half, half), 1)
    near_halo = (((j_h - i_h) * step) >= 0).astype(F32).astype(BF)
    m = lax.broadcasted_iota(jnp.int32, (OUT_T + 2 * HALO_T, OUT_T), 0)
    o = lax.broadcasted_iota(jnp.int32, (OUT_T + 2 * HALO_T, OUT_T), 1)
    window = ((m >= o) & (m <= o + 2 * HALO_T)).astype(F32).astype(BF)
    all_channels = BLK * C
    r_global = lax.broadcasted_iota(jnp.int32, (half, samples), 0) + c * BLK + b * half
    counted = jnp.minimum(r_global, HALO_CH) + jnp.minimum(all_channels - 1 - r_global, HALO_CH) + 1
    per_count = 1.0 / counted.astype(F32)

    @pl.when(jnp.logical_not(has_from))
    def _():
        halo[...] = jnp.zeros_like(halo)

    @pl.when(jnp.logical_not(has_prev))
    def _():
        g_own[...] = jnp.zeros_like(g_own)
        wide[:, :HALO_T] = jnp.zeros((half, HALO_T), BF)

    @pl.when(jnp.logical_not(has_prev & has_from))
    def _():
        g_halo[...] = jnp.zeros_like(g_halo)

    @pl.when(jnp.logical_not(has_next))
    def _():
        wide[:, HALO_T + samples :] = jnp.zeros((half, HALO_T), BF)

    arrived(g_send, g_own, halo_sem.at[1], has_prev)
    arrived(g_send, g_halo, halo_sem.at[2], has_prev & has_from)
    lane0 = lane == 0

    def column(g):
        return jnp.where(lane0, jnp.transpose(jnp.broadcast_to(g[7:8, :], (BLK, BLK))), 0.0)

    fix_own = column(g_own[...])
    fix_halo_all = column(g_halo[...])
    fix_halo = jnp.where(b == 0, fix_halo_all[half:, :], fix_halo_all[:half, :])
    d = deconv[...]
    d = jnp.concatenate([d[:, :BLK] - fix_own, d[:, BLK:]], axis=1)
    d_high, d_low = split(d)
    total = dot(near_own, d_high) + dot(near_own, d_low)
    mine = jnp.where(b == 0, d[:half], d[half:])

    arrived(deconv.at[near], halo, halo_sem.at[0], has_from)
    h = halo[...]
    h = jnp.concatenate([h[:, :BLK] - fix_halo, h[:, BLK:]], axis=1)
    h_high, h_low = split(h)
    total = total + dot(near_halo, h_high) + dot(near_halo, h_low)
    filtered = mine - total * per_count
    filt[...] = filtered
    wide[:, HALO_T : HALO_T + samples] = jnp.abs(filtered).astype(BF)

    start(
        wide.at[:, pl.ds(samples, HALO_T)], wide.at[:, pl.ds(0, HALO_T)],
        time_sem.at[0], {"tm": t_next}, has_next,
    )
    start(
        wide.at[:, pl.ds(HALO_T, HALO_T)], wide.at[:, pl.ds(HALO_T + samples, HALO_T)],
        time_sem.at[1], {"tm": t_prev}, has_prev,
    )

    def normed_blocks(which):
        reach = OUT_T + 2 * HALO_T
        stacked = jnp.concatenate([wide[:, n * OUT_T : n * OUT_T + reach] for n in which], axis=0)
        amp = dot(stacked, window)
        return [
            filt[:, n * OUT_T : (n + 1) * OUT_T]
            / (amp[at * half : (at + 1) * half] * (1.0 / WIN) + 1e-06)
            for at, n in enumerate(which)
        ]

    blocks = samples // OUT_T
    inner = normed_blocks(range(1, blocks - 1))
    fetch.wait()
    arrived(
        wide.at[:, pl.ds(samples, HALO_T)], wide.at[:, pl.ds(0, HALO_T)], time_sem.at[0], has_prev
    )
    arrived(
        wide.at[:, pl.ds(HALO_T, HALO_T)], wide.at[:, pl.ds(HALO_T + samples, HALO_T)],
        time_sem.at[1], has_next,
    )
    first_block, last_block = normed_blocks((0, blocks - 1))
    normed = jnp.concatenate([first_block] + inner + [last_block], axis=1)
    n_high, n_low = split(normed)
    both = dot(jnp.concatenate([n_high, n_low], axis=0), table[0])
    spectrum = both[:half] + both[half:] + dot(n_high, table[1])
    cos_t = share_phase[t, 0:1, :]
    sin_t = share_phase[t, 1:2, :]
    re, im = spectrum[:, :kept], spectrum[:, kept:]
    spec[:, :kept] = (re * cos_t + im * sin_t).astype(BF)
    spec[:, kept:] = (im * cos_t - re * sin_t).astype(BF)

    for n in range(T):
        piece = b * T + n
        t_own, b_own = lax.div(piece, B), lax.rem(piece, B)
        me = (t_own == t) & (b_own == b)

        @pl.when(me)
        def _():
            parts[t] = spec[n * rows : (n + 1) * rows, :]

        start(
            spec.at[pl.ds(n * rows, rows)], parts.at[t], part_sem.at[t],
            {"tm": t_own, "band": b_own}, jnp.logical_not(me),
        )
    own = t * B + b
    b_from = lax.div(own, T)
    for n in range(T):
        arrived(
            spec.at[pl.ds(0, rows)], parts.at[n], part_sem.at[n],
            jnp.logical_not((t == n) & (b_from == b)),
        )
    spectra = parts[0].astype(F32)
    for n in range(1, T):
        spectra = spectra + parts[n].astype(F32)
    power = jnp.sum(spectra * spectra, axis=1, keepdims=True)
    mine_white = (spectra * lax.rsqrt(power * (1.0 / kept) + 1e-06)).astype(BF)
    white[c, own] = mine_white

    def half_of(p, at, h):
        return white.at[p, at, :, pl.ds(h * kept, kept)]

    def block_at(n, sign):
        block = c + sign * n
        return (block >= 0) & (block < C), jnp.clip(block, 0, C - 1)

    for n in (2, 1):
        for h in range(2):
            for sign in (-1, 1):
                there, to = block_at(n, sign)
                piece = half_of(c, own, h)
                start(piece, piece, z_sem.at[h, c], {"chan": to}, there)

    def pass_on(p, sign, h, there):
        piece = half_of(p, own, h)
        goes = (c < C - 1) if sign < 0 else (c > 0)
        to = jnp.clip(c - sign, 0, C - 1)
        start(piece, piece, z_sem.at[h, p], {"chan": to}, there & goes)

    def across(n, sign, h):
        there, p = block_at(n, sign)
        for dt in range(1, T):
            tt = lax.rem(t + dt, T)
            piece = half_of(p, tt * B + b, h)
            arrived(piece, piece, x_sem.at[h, p, tt], there)
            start(piece, piece, c_sem.at[h, p, tt], {"band": 1 - b}, there)

    w = mine_white.astype(F32)
    wr, wi = w[:, :kept], w[:, kept:]
    left = []
    for lag in range(LAGS):
        cos_l = lag_phase[lag, 0:1, :]
        sin_l = lag_phase[lag, 1:2, :]
        left.append(jnp.concatenate([wr * cos_l - wi * sin_l, wr * sin_l + wi * cos_l], axis=1))
    left = jnp.concatenate(left, axis=0).astype(BF)
    steps = [(n, h, sign) for n in [2, 1, *range(3, C)] for h in range(2) for sign in (-1, 1)]
    late = 8
    for at, (n, h, sign) in enumerate(steps):
        there, p = block_at(n, sign)
        piece = half_of(p, own, h)
        arrived(piece, piece, z_sem.at[h, p], there)
        if 2 <= n < C - 1:
            pass_on(p, sign, h, there)
        for dt in range(1, T):
            start(piece, piece, x_sem.at[h, p, t], {"tm": lax.rem(t + dt, T)}, there)
        start(piece, piece, c_sem.at[h, p, t], {"band": 1 - b}, there)
        if at >= late:
            n, h, sign = steps[at - late]
            across(n, sign, h)
    for n, h, sign in steps[max(len(steps) - late, 0):]:
        across(n, sign, h)
    for n, h, sign in steps:
        there, p = block_at(n, sign)
        for tt in range(T):
            piece = half_of(p, tt * B + (1 - b), h)
            arrived(piece, piece, c_sem.at[h, p, tt], there)

    for q in range(QMAX):
        offset = pair[c, q]
        present = offset >= 0
        p = lax.rem(c + jnp.where(present, offset, 1), C)
        right = white[p].reshape(BLK, 2 * kept)
        product = lax.dot_general(left, right, NT, preferred_element_type=F32)
        product = jnp.where(present, product, 0.0)
        for lag in range(LAGS):
            out[0, q, lag] = product[lag * rows : (lag + 1) * rows]

    for copy, cond in sends:
        if cond is None:
            copy.wait_send()
        else:
            pl.when(cond)(copy.wait_send)


def shards(recording, tau_index, pair_offset):
    channels, samples = recording.shape
    C = lax.axis_size("chan")
    T = lax.axis_size("tm")
    B = lax.axis_size("band")
    all_samples = samples * T
    kept = all_samples // 4
    half = BLK // B
    rows = BLK // (T * B)
    table, share_phase, lag_phase = tables(samples, all_samples)
    vmem = pl.BlockSpec(memory_space=pltpu.VMEM)
    n_send = 5 + T + 4 * (C - 1) * (2 * T)
    products = pl.pallas_call(
        functools.partial(kernel, C, T, B),
        out_shape=jax.ShapeDtypeStruct((1, QMAX, LAGS, rows, BLK), F32),
        in_specs=[
            vmem, vmem, pl.BlockSpec(memory_space=pltpu.SMEM),
            pl.BlockSpec(memory_space=pl.ANY), vmem, vmem,
        ],
        out_specs=vmem,
        scratch_shapes=[
            pltpu.VMEM(table.shape, BF),
            pltpu.VMEM((BLK, samples), F32),
            pltpu.VMEM((half, samples), F32),
            pltpu.VMEM((8, BLK), F32),
            pltpu.VMEM((8, BLK), F32),
            pltpu.VMEM((8, BLK), F32),
            pltpu.VMEM((half, samples + 2 * HALO_T), BF),
            pltpu.VMEM((half, samples), F32),
            pltpu.VMEM((half, 2 * kept), BF),
            pltpu.VMEM((T, rows, 2 * kept), BF),
            pltpu.VMEM((C, T * B, rows, 2 * kept), BF),
            pltpu.SemaphoreType.DMA,
            pltpu.SemaphoreType.DMA((n_send,)),
            pltpu.SemaphoreType.DMA((3,)),
            pltpu.SemaphoreType.DMA((2,)),
            pltpu.SemaphoreType.DMA((T,)),
            pltpu.SemaphoreType.DMA((2, C)),
            pltpu.SemaphoreType.DMA((2, C, T)),
            pltpu.SemaphoreType.DMA((2, C, T)),
        ],
        compiler_params=pltpu.CompilerParams(
            collective_id=0, has_side_effects=True, vmem_limit_bytes=61 << 20
        ),
    )(
        recording, tau_index.reshape(1, channels), pair_offset,
        jnp.asarray(table), jnp.asarray(share_phase), jnp.asarray(lag_phase),
    )
    return products * (1.0 / math.sqrt(kept))


def solution(mesh):
    return jax.shard_map(
        shards,
        mesh=mesh,
        in_specs=(P(("groups", "chan"), "tm"), P(("groups", "chan")), P()),
        out_specs=P(("groups", "chan"), None, None, ("tm", "band"), None),
        check_vma=False,
    )
```

```python
import functools
import math

import jax
import jax.numpy as jnp
import ml_dtypes
import numpy as np
from jax import lax
from jax.experimental import pallas as pl
from jax.experimental.pallas import tpu as pltpu
from jax.sharding import PartitionSpec as P

BLK = 128
HALO_CH = 64
HALO_T = 256
LAGS = 3
QMAX = 4
WIN = 2 * HALO_T + 1
OUT_T = 256
BF = jnp.bfloat16
F32 = jnp.float32
NT = (((1,), (1,)), ((), ()))


def tables(samples, all_samples):
    kept = all_samples // 4
    first = kept // 4
    shares = all_samples // samples
    bins = first + np.arange(kept)
    angle = 2.0 * np.pi / all_samples * (np.arange(samples)[:, None] * bins[None, :] % all_samples)
    full = np.concatenate([np.cos(angle), -np.sin(angle)], axis=1).astype(np.float32)
    high = full.astype(ml_dtypes.bfloat16)
    low = (full - high.astype(np.float32)).astype(ml_dtypes.bfloat16)
    turn = 2.0 * np.pi / shares * (np.arange(shares)[:, None] * bins[None, :] % shares)
    share_phase = np.stack([np.cos(turn), np.sin(turn)], axis=1).astype(np.float32)
    lags = np.arange(LAGS) - LAGS // 2
    phase = 2.0 * np.pi / all_samples * (lags[:, None] * bins[None, :] % all_samples)
    lag_phase = np.stack([np.cos(phase), np.sin(phase)], axis=1).astype(np.float32)
    return np.stack([high, low]), share_phase, lag_phase


def split(x):
    high = x.astype(BF)
    return high, (x - high.astype(F32)).astype(BF)


def dot(a, b):
    return jnp.dot(a, b, preferred_element_type=F32)


def kernel(
    C, T, B,
    rec, tau, pair, table_hbm, share_phase, lag_phase, out,
    table, deconv, halo, g_send, g_own, g_halo, wide, filt, spec, parts, white,
    table_sem, send_sem, halo_sem, time_sem, part_sem, z_sem, x_sem, c_sem,
):
    samples = rec.shape[1]
    half = BLK // B
    rows = BLK // (T * B)
    kept = spec.shape[1] // 2
    c = lax.axis_index("chan")
    t = lax.axis_index("tm")
    b = lax.axis_index("band")
    sends = []
    used = [0]

    def remote(src, dst, recv, where, cond=None, at=None):
        if at is None:
            at = used[0]
            used[0] += 1
        copy = pltpu.make_async_remote_copy(
            src_ref=src, dst_ref=dst, send_sem=send_sem.at[at], recv_sem=recv,
            device_id=where, device_id_type=pl.DeviceIdType.MESH,
        )
        return copy, cond

    def start(*args, **kw):
        copy, cond = remote(*args, **kw)
        sends.append((copy, cond))
        if cond is None:
            copy.start()
        else:
            pl.when(cond)(copy.start)

    def arrived(src, dst, recv, cond=None):
        copy, _ = remote(src, dst, recv, {"band": 1 - b}, at=0)
        if cond is None:
            copy.wait_recv()
        else:
            pl.when(cond)(copy.wait_recv)

    fetch = pltpu.make_async_copy(table_hbm, table, table_sem)
    fetch.start()

    barrier = pltpu.get_barrier_semaphore()
    peers = T * B - 1
    for other in range(1, T * B):
        dt, db = divmod(other, B)
        pl.semaphore_signal(
            barrier, inc=1, device_id={"tm": lax.rem(t + dt, T), "band": lax.rem(b + db, B)},
            device_id_type=pl.DeviceIdType.MESH,
        )
    for dc in (-2, -1, 1, 2):
        for dt in (-1, 0, 1) if abs(dc) == 1 else (0,):
            there = (c + dc >= 0) & (c + dc < C) & (t + dt >= 0) & (t + dt < T)
            peers = peers + there.astype(jnp.int32)

            @pl.when(there)
            def _():
                pl.semaphore_signal(
                    barrier, inc=1,
                    device_id={
                        "chan": jnp.clip(c + dc, 0, C - 1), "tm": jnp.clip(t + dt, 0, T - 1)
                    },
                    device_id_type=pl.DeviceIdType.MESH,
                )

    tau_row = 2.0 * jnp.exp(tau[...].astype(F32) * (0.5 * math.log(2.0)))
    decay = jnp.transpose(jnp.broadcast_to(jnp.exp(-1.0 / tau_row), (BLK, BLK)))
    lane = lax.broadcasted_iota(jnp.int32, (BLK, BLK), 1)
    last = rec[:, samples - BLK :]
    g_send[...] = jnp.transpose(decay * last)[BLK - 8 :, :]
    decay_wide = jnp.concatenate([decay] * (samples // BLK), axis=1)
    x = rec[...]
    before = pltpu.roll(x, 1, 1)
    first_col = lax.broadcasted_iota(jnp.int32, x.shape, 1) == 0
    deconv[...] = x - jnp.where(first_col, 0.0, decay_wide * before)

    pl.semaphore_wait(barrier, peers)

    step = 1 - 2 * b
    to_chan = c + step
    from_chan = c - step
    has_to = (to_chan >= 0) & (to_chan < C)
    has_from = (from_chan >= 0) & (from_chan < C)
    to_safe = jnp.clip(to_chan, 0, C - 1)
    near = pl.ds(pl.multiple_of((1 - b) * half, half), half)
    start(deconv.at[near], halo, halo_sem.at[0], {"chan": to_safe}, has_to)
    t_next = jnp.minimum(t + 1, T - 1)
    t_prev = jnp.maximum(t - 1, 0)
    has_next = t < T - 1
    has_prev = t > 0
    start(g_send, g_own, halo_sem.at[1], {"tm": t_next}, has_next)
    start(g_send, g_halo, halo_sem.at[2], {"tm": t_next, "chan": to_safe}, has_next & has_to)

    i_own = lax.broadcasted_iota(jnp.int32, (half, BLK), 0) + b * half
    j_own = lax.broadcasted_iota(jnp.int32, (half, BLK), 1)
    near_own = (jnp.abs(i_own - j_own) <= HALO_CH).astype(F32).astype(BF)
    i_h = lax.broadcasted_iota(jnp.int32, (half, half), 0)
    j_h = lax.broadcasted_iota(jnp.int32, (half, half), 1)
    near_halo = (((j_h - i_h) * step) >= 0).astype(F32).astype(BF)
    m = lax.broadcasted_iota(jnp.int32, (OUT_T + 2 * HALO_T, OUT_T), 0)
    o = lax.broadcasted_iota(jnp.int32, (OUT_T + 2 * HALO_T, OUT_T), 1)
    window = ((m >= o) & (m <= o + 2 * HALO_T)).astype(F32).astype(BF)
    all_channels = BLK * C
    r_global = lax.broadcasted_iota(jnp.int32, (half, samples), 0) + c * BLK + b * half
    counted = jnp.minimum(r_global, HALO_CH) + jnp.minimum(all_channels - 1 - r_global, HALO_CH) + 1
    per_count = 1.0 / counted.astype(F32)

    @pl.when(jnp.logical_not(has_from))
    def _():
        halo[...] = jnp.zeros_like(halo)

    @pl.when(jnp.logical_not(has_prev))
    def _():
        g_own[...] = jnp.zeros_like(g_own)
        wide[:, :HALO_T] = jnp.zeros((half, HALO_T), BF)

    @pl.when(jnp.logical_not(has_prev & has_from))
    def _():
        g_halo[...] = jnp.zeros_like(g_halo)

    @pl.when(jnp.logical_not(has_next))
    def _():
        wide[:, HALO_T + samples :] = jnp.zeros((half, HALO_T), BF)

    arrived(g_send, g_own, halo_sem.at[1], has_prev)
    arrived(g_send, g_halo, halo_sem.at[2], has_prev & has_from)
    lane0 = lane == 0

    def column(g):
        return jnp.where(lane0, jnp.transpose(jnp.broadcast_to(g[7:8, :], (BLK, BLK))), 0.0)

    fix_own = column(g_own[...])
    fix_halo_all = column(g_halo[...])
    fix_halo = jnp.where(b == 0, fix_halo_all[half:, :], fix_halo_all[:half, :])
    d = deconv[...]
    d = jnp.concatenate([d[:, :BLK] - fix_own, d[:, BLK:]], axis=1)
    d_high, d_low = split(d)
    total = dot(near_own, d_high) + dot(near_own, d_low)
    mine = jnp.where(b == 0, d[:half], d[half:])

    arrived(deconv.at[near], halo, halo_sem.at[0], has_from)
    h = halo[...]
    h = jnp.concatenate([h[:, :BLK] - fix_halo, h[:, BLK:]], axis=1)
    h_high, h_low = split(h)
    total = total + dot(near_halo, h_high) + dot(near_halo, h_low)
    filtered = mine - total * per_count
    filt[...] = filtered
    wide[:, HALO_T : HALO_T + samples] = jnp.abs(filtered).astype(BF)

    start(
        wide.at[:, pl.ds(samples, HALO_T)], wide.at[:, pl.ds(0, HALO_T)],
        time_sem.at[0], {"tm": t_next}, has_next,
    )
    start(
        wide.at[:, pl.ds(HALO_T, HALO_T)], wide.at[:, pl.ds(HALO_T + samples, HALO_T)],
        time_sem.at[1], {"tm": t_prev}, has_prev,
    )

    def normed_blocks(which):
        reach = OUT_T + 2 * HALO_T
        stacked = jnp.concatenate([wide[:, n * OUT_T : n * OUT_T + reach] for n in which], axis=0)
        amp = dot(stacked, window)
        return [
            filt[:, n * OUT_T : (n + 1) * OUT_T]
            / (amp[at * half : (at + 1) * half] * (1.0 / WIN) + 1e-06)
            for at, n in enumerate(which)
        ]

    blocks = samples // OUT_T
    inner = normed_blocks(range(1, blocks - 1))
    fetch.wait()

    def transform(high, low, at):
        size = high.shape[1]
        both = dot(jnp.concatenate([high, low], axis=0), table[0, at : at + size])
        return both[:half] + both[half:] + dot(high, table[1, at : at + size])

    inner_high, inner_low = split(jnp.concatenate(inner, axis=1))
    spectrum = transform(inner_high, inner_low, OUT_T)
    arrived(
        wide.at[:, pl.ds(samples, HALO_T)], wide.at[:, pl.ds(0, HALO_T)], time_sem.at[0], has_prev
    )
    arrived(
        wide.at[:, pl.ds(HALO_T, HALO_T)], wide.at[:, pl.ds(HALO_T + samples, HALO_T)],
        time_sem.at[1], has_next,
    )
    first_block, last_block = normed_blocks((0, blocks - 1))
    spectrum = spectrum + transform(*split(first_block), 0)
    spectrum = spectrum + transform(*split(last_block), samples - OUT_T)
    cos_t = share_phase[t, 0:1, :]
    sin_t = share_phase[t, 1:2, :]
    re, im = spectrum[:, :kept], spectrum[:, kept:]
    spec[:, :kept] = (re * cos_t + im * sin_t).astype(BF)
    spec[:, kept:] = (im * cos_t - re * sin_t).astype(BF)

    for n in range(T):
        piece = b * T + n
        t_own, b_own = lax.div(piece, B), lax.rem(piece, B)
        me = (t_own == t) & (b_own == b)

        @pl.when(me)
        def _():
            parts[t] = spec[n * rows : (n + 1) * rows, :]

        start(
            spec.at[pl.ds(n * rows, rows)], parts.at[t], part_sem.at[t],
            {"tm": t_own, "band": b_own}, jnp.logical_not(me),
        )
    own = t * B + b
    b_from = lax.div(own, T)
    for n in range(T):
        arrived(
            spec.at[pl.ds(0, rows)], parts.at[n], part_sem.at[n],
            jnp.logical_not((t == n) & (b_from == b)),
        )
    spectra = parts[0].astype(F32)
    for n in range(1, T):
        spectra = spectra + parts[n].astype(F32)
    power = jnp.sum(spectra * spectra, axis=1, keepdims=True)
    mine_white = (spectra * lax.rsqrt(power * (1.0 / kept) + 1e-06)).astype(BF)
    white[c, own] = mine_white

    def half_of(p, at, h):
        return white.at[p, at, :, pl.ds(h * kept, kept)]

    def block_at(n, sign):
        block = c + sign * n
        return (block >= 0) & (block < C), jnp.clip(block, 0, C - 1)

    for n in (2, 1):
        for h in range(2):
            for sign in (-1, 1):
                there, to = block_at(n, sign)
                piece = half_of(c, own, h)
                start(piece, piece, z_sem.at[h, c], {"chan": to}, there)

    def pass_on(p, sign, h, there):
        piece = half_of(p, own, h)
        goes = (c < C - 1) if sign < 0 else (c > 0)
        to = jnp.clip(c - sign, 0, C - 1)
        start(piece, piece, z_sem.at[h, p], {"chan": to}, there & goes)

    def across(n, sign, h):
        there, p = block_at(n, sign)
        for dt in range(1, T):
            tt = lax.rem(t + dt, T)
            piece = half_of(p, tt * B + b, h)
            arrived(piece, piece, x_sem.at[h, p, tt], there)
            start(piece, piece, c_sem.at[h, p, tt], {"band": 1 - b}, there)

    w = mine_white.astype(F32)
    wr, wi = w[:, :kept], w[:, kept:]
    left = []
    for lag in range(LAGS):
        cos_l = lag_phase[lag, 0:1, :]
        sin_l = lag_phase[lag, 1:2, :]
        left.append(jnp.concatenate([wr * cos_l - wi * sin_l, wr * sin_l + wi * cos_l], axis=1))
    left = jnp.concatenate(left, axis=0).astype(BF)
    steps = [(n, h, sign) for n in [2, 1, *range(3, C)] for h in range(2) for sign in (-1, 1)]
    late = 8
    for at, (n, h, sign) in enumerate(steps):
        there, p = block_at(n, sign)
        piece = half_of(p, own, h)
        arrived(piece, piece, z_sem.at[h, p], there)
        if 2 <= n < C - 1:
            pass_on(p, sign, h, there)
        for dt in range(1, T):
            start(piece, piece, x_sem.at[h, p, t], {"tm": lax.rem(t + dt, T)}, there)
        start(piece, piece, c_sem.at[h, p, t], {"band": 1 - b}, there)
        if at >= late:
            n, h, sign = steps[at - late]
            across(n, sign, h)
    for n, h, sign in steps[max(len(steps) - late, 0):]:
        across(n, sign, h)
    for n, h, sign in steps:
        there, p = block_at(n, sign)
        for tt in range(T):
            piece = half_of(p, tt * B + (1 - b), h)
            arrived(piece, piece, c_sem.at[h, p, tt], there)

    for q in range(QMAX):
        offset = pair[c, q]
        present = offset >= 0
        p = lax.rem(c + jnp.where(present, offset, 1), C)
        right = white[p].reshape(BLK, 2 * kept)
        product = lax.dot_general(left, right, NT, preferred_element_type=F32)
        product = jnp.where(present, product, 0.0)
        for lag in range(LAGS):
            out[0, q, lag] = product[lag * rows : (lag + 1) * rows]

    for copy, cond in sends:
        if cond is None:
            copy.wait_send()
        else:
            pl.when(cond)(copy.wait_send)


def shards(recording, tau_index, pair_offset):
    channels, samples = recording.shape
    C = lax.axis_size("chan")
    T = lax.axis_size("tm")
    B = lax.axis_size("band")
    all_samples = samples * T
    kept = all_samples // 4
    half = BLK // B
    rows = BLK // (T * B)
    table, share_phase, lag_phase = tables(samples, all_samples)
    vmem = pl.BlockSpec(memory_space=pltpu.VMEM)
    n_send = 5 + T + 4 * (C - 1) * (2 * T)
    products = pl.pallas_call(
        functools.partial(kernel, C, T, B),
        out_shape=jax.ShapeDtypeStruct((1, QMAX, LAGS, rows, BLK), F32),
        in_specs=[
            vmem, vmem, pl.BlockSpec(memory_space=pltpu.SMEM),
            pl.BlockSpec(memory_space=pl.ANY), vmem, vmem,
        ],
        out_specs=vmem,
        scratch_shapes=[
            pltpu.VMEM(table.shape, BF),
            pltpu.VMEM((BLK, samples), F32),
            pltpu.VMEM((half, samples), F32),
            pltpu.VMEM((8, BLK), F32),
            pltpu.VMEM((8, BLK), F32),
            pltpu.VMEM((8, BLK), F32),
            pltpu.VMEM((half, samples + 2 * HALO_T), BF),
            pltpu.VMEM((half, samples), F32),
            pltpu.VMEM((half, 2 * kept), BF),
            pltpu.VMEM((T, rows, 2 * kept), BF),
            pltpu.VMEM((C, T * B, rows, 2 * kept), BF),
            pltpu.SemaphoreType.DMA,
            pltpu.SemaphoreType.DMA((n_send,)),
            pltpu.SemaphoreType.DMA((3,)),
            pltpu.SemaphoreType.DMA((2,)),
            pltpu.SemaphoreType.DMA((T,)),
            pltpu.SemaphoreType.DMA((2, C)),
            pltpu.SemaphoreType.DMA((2, C, T)),
            pltpu.SemaphoreType.DMA((2, C, T)),
        ],
        compiler_params=pltpu.CompilerParams(
            collective_id=0, has_side_effects=True, vmem_limit_bytes=61 << 20
        ),
    )(
        recording, tau_index.reshape(1, channels), pair_offset,
        jnp.asarray(table), jnp.asarray(share_phase), jnp.asarray(lag_phase),
    )
    return products * (1.0 / math.sqrt(kept))


def solution(mesh):
    return jax.shard_map(
        shards,
        mesh=mesh,
        in_specs=(P(("groups", "chan"), "tm"), P(("groups", "chan")), P()),
        out_specs=P(("groups", "chan"), None, None, ("tm", "band"), None),
        check_vma=False,
    )
```
